256 devices in a mesh: rows: 64 (over z, x, core), grp: 4 (over y).
Axes of the slice: x: 4, y: 4, z: 8, core: 2. Of those that a mesh axis runs over, the one named last changes fastest.
Arguments:
- inputs: bfloat16 [262144, 128], P(('rows', 'grp')), may hold values from -6 to 6
- near_tiles: bfloat16 [1024, 256, 4096], P(('rows', 'grp')), may hold values from -0.09375 to 0.09375
- far_left: bfloat16 [16384, 256, 32], P(('rows', 'grp')), may hold values from -0.25 to 0.25
- far_right: bfloat16 [16384, 256, 32], P(('rows', 'grp')), may hold values from -0.375 to 0.375
- far_rows: int32 [16384], P(('rows', 'grp')), may hold values from 0 to 3
- far_cols: int32 [16384], P(('rows', 'grp')), may hold values from 0 to 3
- far_rank: int32 [16384], P(('rows', 'grp')), may hold values from 1 to 32
Outputs:
- product: float32 [262144, 128], P(('rows', 'grp'))
The draws below stay inside these ranges and needn't reach their ends.
All inputs are finite; a program needn't handle non-finite values.
Results may differ from the reference program's by a relative error of at most 0.0018.
Values may be sent and summed in bfloat16 or wider, within the bound.
No kernel may reach another device: no remote copies, remote signals or barrier semaphores. Data moves between devices by JAX's collectives and lax.ppermute only.
A program may use at most 64 MiB of HBM per device.

```python
import jax
import jax.numpy as jnp
from jax import lax

NRHS = 128
R = 32
CS = 256
CL_DEV = 4
CAP = 1
SLOT_DEV = 64
SLOTS = 16384
GROUP_COLS = 4096
NC = 1024
N = 262144
N_ROWS = 64
N_GRP = 4


def plant(array, stream_key, low, largest):
    spot = [jax.random.randint(jax.random.fold_in(stream_key, axis), (), 0, length) for axis, length in enumerate(array.shape)]
    main_axis = array.shape.index(max(array.shape))
    beside = spot[:main_axis] + [(spot[main_axis] + 1) % array.shape[main_axis]] + spot[main_axis + 1:]
    return array.at[tuple(spot)].set(low).at[tuple(beside)].set(largest)


def shard_levels(stream_key, extent, shards, low, top_value):
    level = 1.0
    for dim, shards_of in shards:
        heights = jax.random.uniform(jax.random.fold_in(jax.random.fold_in(stream_key, 6), dim), (shards_of,), jnp.float32, low / len(shards), top_value / len(shards))
        level = level * jnp.repeat(jnp.exp(heights), extent[dim] // shards_of).reshape((-1,) + (1,) * (len(extent) - 1 - dim))
    return level


def normal_values(rng, extent, scale, most, cuts=(), kind=jnp.bfloat16):
    values = scale * jax.random.normal(rng, extent, jnp.float32)
    if cuts:
        values = values * shard_levels(rng, extent, cuts, -0.22, 0.18)
    return jnp.clip(values, -most, most).astype(kind)


def setup_inputs(seed: int = 0) -> dict:
    keys = jax.random.split(jax.random.key(seed), 8)
    inputs = normal_values(keys[0], (N, NRHS), 1.0, 6.0, ((0, 256),))
    near_tiles = normal_values(keys[1], (NC, CS, GROUP_COLS), GROUP_COLS ** -0.5, 0.09375, ((0, 256),))
    far_left = normal_values(keys[2], (SLOTS, CS, R), (R * SLOT_DEV // CL_DEV) ** -0.5, 0.25, ((0, 256),))
    far_right = normal_values(keys[3], (SLOTS, CS, R), CS ** -0.5, 0.375, ((0, 256),))
    far_rows = plant(jax.random.randint(keys[4], (SLOTS,), 0, CL_DEV), jax.random.fold_in(keys[4], 1), 0, CL_DEV - 1).astype(jnp.int32)
    far_cols = plant(jax.random.randint(keys[5], (SLOTS,), 0, CL_DEV), jax.random.fold_in(keys[5], 1), 0, CL_DEV - 1).astype(jnp.int32)
    far_rank = plant(jax.random.randint(keys[6], (SLOTS,), 1, R + 1), jax.random.fold_in(keys[6], 1), 1, R).astype(jnp.int32)
    return {"inputs": inputs, "near_tiles": near_tiles, "far_left": far_left, "far_right": far_right, "far_rows": far_rows, "far_cols": far_cols, "far_rank": far_rank}


def reference(inputs, near_tiles, far_left, far_right, far_rows, far_cols, far_rank):
    devices = N_ROWS * N_GRP
    tiles = near_tiles.reshape(N_ROWS, N_GRP * CL_DEV * CS, GROUP_COLS)
    grouped = inputs.reshape(N_ROWS, GROUP_COLS, NRHS)

    def near_group(pair):
        return jnp.dot(pair[0], pair[1], preferred_element_type=jnp.float32)

    near = lax.map(near_group, (tiles, grouped)).reshape(N, NRHS)
    clusters = inputs.reshape(NC, CS, NRHS)

    def far_device(packed):
        device, left, right, rows_of, cols_of, ranks = packed
        group_pos = device % N_GRP
        peer = jnp.arange(SLOT_DEV, dtype=jnp.int32) // CAP
        column = (peer * N_GRP + group_pos) * CL_DEV + cols_of
        picked = jnp.take(clusters, column.astype(jnp.int32), axis=0)
        coeff = jnp.einsum("sir,sin->srn", right.astype(jnp.float32), picked.astype(jnp.float32))
        coeff = coeff.astype(jnp.bfloat16)
        keep = jnp.arange(R, dtype=jnp.int32)[None, :] < ranks[:, None]
        coeff = jnp.where(keep[:, :, None], coeff, jnp.zeros_like(coeff))
        onehot = (rows_of[:, None] == jnp.arange(CL_DEV, dtype=jnp.int32)[None, :]).astype(jnp.float32)
        spread = onehot.T[:, :, None, None] * coeff.astype(jnp.float32)[None]
        return jnp.einsum("sir,csrn->cin", left.astype(jnp.float32), spread)

    packed = (jnp.arange(devices, dtype=jnp.int32),
              far_left.reshape(devices, SLOT_DEV, CS, R),
              far_right.reshape(devices, SLOT_DEV, CS, R),
              far_rows.reshape(devices, SLOT_DEV),
              far_cols.reshape(devices, SLOT_DEV),
              far_rank.reshape(devices, SLOT_DEV))
    far = lax.map(far_device, packed).reshape(N, NRHS)
    return near + far
```

```python
import functools

import jax
import jax.numpy as jnp
from jax import lax
from jax.experimental import pallas as pl
from jax.experimental.pallas import tpu as pltpu
from jax.sharding import Mesh, PartitionSpec as P

NZ, NX, NCORE = 8, 4, 2
PEERS = NX * NCORE
PLANE = ("x", "core")
VMEM_LIMIT = 48 * 1024 * 1024


def vmem():
    return pl.BlockSpec(memory_space=pltpu.VMEM)


def smem():
    return pl.BlockSpec(memory_space=pltpu.SMEM)


def call(kernel, out, in_specs, scratch=()):
    return pl.pallas_call(
        kernel,
        out_shape=out,
        in_specs=in_specs,
        out_specs=vmem(),
        scratch_shapes=list(scratch),
        compiler_params=pltpu.CompilerParams(vmem_limit_bytes=VMEM_LIMIT),
    )


def pack_kernel(z_ref, cols_ref, right_ref, out_ref):
    z = z_ref[0]
    rank = right_ref.shape[1]
    width = right_ref.shape[2]
    row = lax.broadcasted_iota(jnp.int32, (16, width), 0)
    for p in range(PEERS):
        tail = jnp.zeros((16, width), jnp.float32)
        for k in range(NZ):
            slot = lax.rem(z + k, NZ) * PEERS + p
            out_ref[p, k * rank : (k + 1) * rank, :] = right_ref[slot]
            tail = jnp.where(row == k, cols_ref[slot].astype(jnp.float32), tail)
        out_ref[p, NZ * rank : NZ * rank + 16, :] = tail.astype(jnp.bfloat16)


def coeff_kernel(ks, rank, msg_ref, *refs):
    chunk_refs, out_ref = refs[:-1], refs[-1]
    n_clusters = chunk_refs[0].shape[0] // msg_ref.shape[2]
    size = msg_ref.shape[2]
    tails = [msg_ref[p, NZ * rank : NZ * rank + 16, :].astype(jnp.float32) for p in range(PEERS)]
    for j, k in enumerate(ks):
        total = None
        for c in range(n_clusters):
            parts = []
            for p in range(PEERS):
                pick = (tails[p][k : k + 1, :] == c).astype(jnp.bfloat16)
                parts.append(msg_ref[p, k * rank : (k + 1) * rank, :] * pick)
            term = jnp.dot(
                jnp.concatenate(parts, axis=0),
                chunk_refs[j][c * size : (c + 1) * size, :],
                preferred_element_type=jnp.float32,
            )
            total = term if total is None else total + term
        total = total.astype(jnp.bfloat16)
        for p in range(PEERS):
            out_ref[p, j * rank : (j + 1) * rank, :] = total[p * rank : (p + 1) * rank, :]


def far_kernel(ks, z_ref, rows_ref, ranks_ref, left_ref, coeff_ref, near_ref, out_ref, spread_ref):
    z = z_ref[0]
    n_slots, rank, size = left_ref.shape
    n_rhs = coeff_ref.shape[2]
    n_clusters = near_ref.shape[0] // size
    index = lax.broadcasted_iota(jnp.int32, (rank, n_rhs), 0)
    for p in range(PEERS):
        for j, k in enumerate(ks):
            slot = lax.rem(z + k, NZ) * PEERS + p
            block = coeff_ref[p, j * rank : (j + 1) * rank, :].astype(jnp.float32)
            block = jnp.where(index < ranks_ref[slot], block, 0.0)
            start = pl.multiple_of(slot * rank, rank)
            for c in range(n_clusters):
                here = jnp.where(rows_ref[slot] == c, block, 0.0)
                spread_ref[pl.ds(start, rank), c * n_rhs : (c + 1) * n_rhs] = here.astype(jnp.bfloat16)
    far = lax.dot_general(
        left_ref[...].reshape(n_slots * rank, size),
        spread_ref[...],
        (((0,), (0,)), ((), ())),
        preferred_element_type=jnp.float32,
    )
    for c in range(n_clusters):
        rows = slice(c * size, (c + 1) * size)
        out_ref[rows, :] = near_ref[rows, :] + far[:, c * n_rhs : (c + 1) * n_rhs]


def shift(a, axis, step, size):
    return lax.ppermute(a, axis, [(i, (i + step) % size) for i in range(size)])


def local(n_grp, inputs, near_tiles, far_left, far_right, far_rows, far_cols, far_rank):
    n_clusters, size, width_cols = near_tiles.shape
    unknowns, n_rhs = inputs.shape
    n_slots, _, rank = far_left.shape
    z = lax.axis_index("z").astype(jnp.int32).reshape(1)

    packed = call(
        pack_kernel,
        jax.ShapeDtypeStruct((PEERS, NZ * rank + 16, size), jnp.bfloat16),
        [smem(), smem(), vmem()],
    )(z, far_cols, jnp.swapaxes(far_right, 1, 2))
    msg = lax.all_to_all(packed, PLANE, 0, 0, tiled=True)

    chunks = {0: inputs}
    up = down = inputs
    for step in range(1, NZ // 2 + 1):
        up = shift(up, "z", 1, NZ)
        chunks[NZ - step] = up
        if step < NZ // 2:
            down = shift(down, "z", -1, NZ)
            chunks[step] = down

    y = lax.axis_index("grp")
    gathered = jnp.zeros((width_cols, n_rhs), jnp.bfloat16)
    beside = inputs
    for step in range(n_grp):
        if step:
            beside = shift(beside, "grp", 1, n_grp)
        gathered = lax.dynamic_update_slice(gathered, beside, (((y - step) % n_grp) * unknowns, 0))
    near = jnp.dot(
        near_tiles.reshape(unknowns, width_cols), gathered, preferred_element_type=jnp.float32
    )

    ks = tuple(range(NZ))
    coeff = call(
        functools.partial(coeff_kernel, ks, rank),
        jax.ShapeDtypeStruct((PEERS, len(ks) * rank, n_rhs), jnp.bfloat16),
        [vmem()] * (1 + len(ks)),
    )(msg, *[chunks[k] for k in ks])
    back = lax.all_to_all(coeff, PLANE, 0, 0, tiled=True)
    return call(
        functools.partial(far_kernel, ks),
        jax.ShapeDtypeStruct((unknowns, n_rhs), jnp.float32),
        [smem(), smem(), smem(), vmem(), vmem(), vmem()],
        [pltpu.VMEM((n_slots * rank, n_clusters * n_rhs), jnp.bfloat16)],
    )(z, far_rows, far_rank, jnp.swapaxes(far_left, 1, 2), back, near)


def solution(mesh):
    n_grp = mesh.shape["grp"]
    fine = Mesh(mesh.devices.reshape(NZ, NX, NCORE, n_grp), ("z", "x", "core", "grp"))
    spec = P(("z", "x", "core", "grp"))
    return jax.shard_map(
        functools.partial(local, n_grp), mesh=fine, in_specs=(spec,) * 7, out_specs=spec, check_vma=False
    )
```

```python
import functools

import jax
import jax.numpy as jnp
from jax import lax
from jax.experimental import pallas as pl
from jax.experimental.pallas import tpu as pltpu
from jax.sharding import Mesh, PartitionSpec as P

NZ, NX, NCORE = 8, 4, 2
PEERS = NX * NCORE
PLANE = ("x", "core")
FIRST, LAST = (0, 7, 1, 6, 2), (5, 3, 4)
VMEM_LIMIT = 16 * 1024 * 1024


def slot_of(z, k, peer):
    step = k * (1 - 2 * lax.rem(z, 2))
    return lax.rem(z + step + NZ, NZ) * PEERS + peer


def vmem():
    return pl.BlockSpec(memory_space=pltpu.VMEM)


def smem():
    return pl.BlockSpec(memory_space=pltpu.SMEM)


def call(kernel, out, in_specs, scratch=(), flops=0):
    return pl.pallas_call(
        kernel,
        out_shape=out,
        in_specs=in_specs,
        out_specs=vmem(),
        scratch_shapes=list(scratch),
        compiler_params=pltpu.CompilerParams(vmem_limit_bytes=VMEM_LIMIT),
        cost_estimate=pl.CostEstimate(flops=flops, bytes_accessed=0, transcendentals=0) if flops else None,
    )


def pack_kernel(z_ref, cols_ref, right_ref, out_ref):
    z = z_ref[0]
    rank = right_ref.shape[1]
    width = right_ref.shape[2]
    row = lax.broadcasted_iota(jnp.int32, (16, width), 0)
    for p in range(PEERS):
        tail = jnp.zeros((16, width), jnp.float32)
        for k in range(NZ):
            slot = slot_of(z, k, p)
            out_ref[p, k * rank : (k + 1) * rank, :] = right_ref[slot]
            tail = jnp.where(row == k, cols_ref[slot].astype(jnp.float32), tail)
        out_ref[p, NZ * rank : NZ * rank + 16, :] = tail.astype(jnp.bfloat16)


def coeff_block(msg_ref, chunk_ref, tails, k, rank):
    size = msg_ref.shape[2]
    total = None
    for c in range(chunk_ref.shape[0] // size):
        parts = []
        for p in range(PEERS):
            pick = (tails[p][k : k + 1, :] == c).astype(jnp.bfloat16)
            parts.append(msg_ref[p, k * rank : (k + 1) * rank, :] * pick)
        term = jnp.dot(
            jnp.concatenate(parts, axis=0),
            chunk_ref[c * size : (c + 1) * size, :],
            preferred_element_type=jnp.float32,
        )
        total = term if total is None else total + term
    return total.astype(jnp.bfloat16)


def coeff_kernel(early, ks, rank, msg_ref, *refs):
    out_ref = refs[-1]
    if early:
        for p in range(PEERS):
            out_ref[p, : len(early) * rank, :] = refs[0][p]
        refs = refs[1:]
    tails = [msg_ref[p, NZ * rank :, :].astype(jnp.float32) for p in range(PEERS)]
    for j, k in enumerate(ks):
        block = coeff_block(msg_ref, refs[j], tails, k, rank)
        at = (len(early) + j) * rank
        for p in range(PEERS):
            out_ref[p, at : at + rank, :] = block[p * rank : (p + 1) * rank, :]


def far_kernel(ks, z_ref, rows_ref, ranks_ref, left_ref, coeff_ref, near_ref, out_ref, spread_ref):
    z = z_ref[0]
    n_slots, rank, size = left_ref.shape
    n_rhs = coeff_ref.shape[2]
    n_clusters = near_ref.shape[0] // size
    index = lax.broadcasted_iota(jnp.int32, (rank, n_rhs), 0)
    for p in range(PEERS):
        for j, k in enumerate(ks):
            slot = slot_of(z, k, p)
            block = coeff_ref[p, j * rank : (j + 1) * rank, :].astype(jnp.float32)
            block = jnp.where(index < ranks_ref[slot], block, 0.0)
            start = pl.multiple_of(slot * rank, rank)
            for c in range(n_clusters):
                here = jnp.where(rows_ref[slot] == c, block, 0.0)
                spread_ref[pl.ds(start, rank), c * n_rhs : (c + 1) * n_rhs] = here.astype(jnp.bfloat16)
    far = lax.dot_general(
        left_ref[...].reshape(n_slots * rank, size),
        spread_ref[...],
        (((0,), (0,)), ((), ())),
        preferred_element_type=jnp.float32,
    )
    for c in range(n_clusters):
        rows = slice(c * size, (c + 1) * size)
        out_ref[rows, :] = near_ref[rows, :] + far[:, c * n_rhs : (c + 1) * n_rhs]


def near_kernel(y_ref, tiles_ref, *refs):
    chunk_refs, (out_ref, held_ref, sems) = refs[:-3], refs[-3:]
    width = chunk_refs[0].shape[0]
    sign = 1 - 2 * lax.rem(y_ref[0], 2)
    n_blocks, rows, _ = held_ref.shape
    copies = [
        pltpu.make_async_copy(tiles_ref.at[pl.ds(b * rows, rows), :], held_ref.at[b], sems.at[b])
        for b in range(n_blocks)
    ]
    for copy in copies:
        copy.start()
    for b, copy in enumerate(copies):
        copy.wait()
        total = None
        for step, chunk_ref in enumerate(chunk_refs):
            column = pl.multiple_of(lax.rem(y_ref[0] + step * sign + len(chunk_refs), len(chunk_refs)) * width, width)
            term = jnp.dot(
                held_ref[b, :, pl.ds(column, width)], chunk_ref[...], preferred_element_type=jnp.float32
            )
            total = term if total is None else total + term
        out_ref[b * rows : (b + 1) * rows, :] = total


def swap(a, axis, size, odd):
    return lax.ppermute(a, axis, [(i, (i + (1 if i % 2 == odd else -1)) % size) for i in range(size)])


def local(n_grp, inputs, near_tiles, far_left, far_right, far_rows, far_cols, far_rank):
    n_clusters, size, width_cols = near_tiles.shape
    unknowns, n_rhs = inputs.shape
    n_slots, _, rank = far_left.shape
    z = lax.axis_index("z").astype(jnp.int32).reshape(1)

    chunks, one, two = {0: inputs}, inputs, inputs
    for step in range(1, NZ // 2 + 1):
        one = swap(one, "z", NZ, (step + 1) % 2)
        chunks[step if step % 2 else NZ - step] = one
        if step < NZ // 2:
            two = swap(two, "z", NZ, step % 2)
            chunks[NZ - step if step % 2 else step] = two
        if step == 2:
            one, two, held = lax.optimization_barrier((one, two, inputs))
            beside = [inputs, swap(held, "grp", n_grp, 0), None, swap(held, "grp", n_grp, 1)]
            beside[2] = swap(beside[3], "grp", n_grp, 0)
        elif step < NZ // 2:
            one, two = lax.optimization_barrier((one, two))

    packed = call(
        pack_kernel,
        jax.ShapeDtypeStruct((PEERS, NZ * rank + 16, size), jnp.bfloat16),
        [smem(), smem(), vmem()],
    )(z, far_cols, jnp.swapaxes(far_right, 1, 2))
    msg = lax.all_to_all(packed, PLANE, 0, 0, tiled=True)

    y = lax.axis_index("grp").astype(jnp.int32).reshape(1)
    coeff = []
    for early, ks in (((), FIRST), (FIRST, LAST)):
        depth = (len(early) + len(ks)) * rank
        coeff = [
            call(
                functools.partial(coeff_kernel, early, ks, rank),
                jax.ShapeDtypeStruct((PEERS, depth, n_rhs), jnp.bfloat16),
                [vmem()] * (1 + len(coeff) + len(ks)),
            )(msg, *coeff, *[chunks[k] for k in ks])
        ]
    back = lax.all_to_all(coeff[0], PLANE, 0, 0, tiled=True)

    row_block = 256
    near = call(
        near_kernel,
        jax.ShapeDtypeStruct((unknowns, n_rhs), jnp.float32),
        [smem(), pl.BlockSpec(memory_space=pltpu.HBM)] + [vmem()] * n_grp,
        [
            pltpu.VMEM((unknowns // row_block, row_block, width_cols), jnp.bfloat16),
            pltpu.SemaphoreType.DMA((unknowns // row_block,)),
        ],
        flops=3 * 10**10,
    )(y, near_tiles.reshape(unknowns, width_cols), *beside)
    return call(
        functools.partial(far_kernel, FIRST + LAST),
        jax.ShapeDtypeStruct((unknowns, n_rhs), jnp.float32),
        [smem(), smem(), smem(), vmem(), vmem(), vmem()],
        [pltpu.VMEM((n_slots * rank, n_clusters * n_rhs), jnp.bfloat16)],
    )(z, far_rows, far_rank, jnp.swapaxes(far_left, 1, 2), back, near)


def solution(mesh):
    n_grp = mesh.shape["grp"]
    fine = Mesh(mesh.devices.reshape(NZ, NX, NCORE, n_grp), ("z", "x", "core", "grp"))
    spec = P(("z", "x", "core", "grp"))
    return jax.shard_map(
        functools.partial(local, n_grp), mesh=fine, in_specs=(spec,) * 7, out_specs=spec, check_vma=False
    )
```

```python
import functools

import jax
import jax.numpy as jnp
from jax import lax
from jax.experimental import pallas as pl
from jax.experimental.pallas import tpu as pltpu
from jax.sharding import Mesh, PartitionSpec as P

NZ, NX, NCORE = 8, 4, 2
PEERS = NX * NCORE
PLANE = ("x", "core")
FIRST, LAST = (0, 7, 1, 6, 2, 5, 3), (4,)
VMEM_LIMIT = 16 * 1024 * 1024


def slot_of(z, k, peer):
    step = k * (1 - 2 * lax.rem(z, 2))
    return lax.rem(z + step + NZ, NZ) * PEERS + peer


def vmem():
    return pl.BlockSpec(memory_space=pltpu.VMEM)


def smem():
    return pl.BlockSpec(memory_space=pltpu.SMEM)


def call(kernel, out, in_specs, scratch=(), flops=0):
    return pl.pallas_call(
        kernel,
        out_shape=out,
        in_specs=in_specs,
        out_specs=vmem(),
        scratch_shapes=list(scratch),
        compiler_params=pltpu.CompilerParams(vmem_limit_bytes=VMEM_LIMIT),
        cost_estimate=pl.CostEstimate(flops=flops, bytes_accessed=0, transcendentals=0) if flops else None,
    )


def pack_kernel(z_ref, cols_ref, right_ref, out_ref):
    z = z_ref[0]
    rank = right_ref.shape[1]
    width = right_ref.shape[2]
    row = lax.broadcasted_iota(jnp.int32, (16, width), 0)
    for p in range(PEERS):
        tail = jnp.zeros((16, width), jnp.float32)
        for k in range(NZ):
            slot = slot_of(z, k, p)
            out_ref[p, k * rank : (k + 1) * rank, :] = right_ref[slot]
            tail = jnp.where(row == k, cols_ref[slot].astype(jnp.float32), tail)
        out_ref[p, NZ * rank : NZ * rank + 16, :] = tail.astype(jnp.bfloat16)


def coeff_block(msg_ref, chunk_ref, tails, k, rank):
    size = msg_ref.shape[2]
    total = None
    for c in range(chunk_ref.shape[0] // size):
        parts = []
        for p in range(PEERS):
            pick = (tails[p][k : k + 1, :] == c).astype(jnp.bfloat16)
            parts.append(msg_ref[p, k * rank : (k + 1) * rank, :] * pick)
        term = jnp.dot(
            jnp.concatenate(parts, axis=0),
            chunk_ref[c * size : (c + 1) * size, :],
            preferred_element_type=jnp.float32,
        )
        total = term if total is None else total + term
    return total.astype(jnp.bfloat16)


def first_coeff_kernel(rank, msg_ref, *refs):
    chunk_refs, out_ref = refs[:-1], refs[-1]
    tails = [msg_ref[p, NZ * rank :, :].astype(jnp.float32) for p in range(PEERS)]
    for j, k in enumerate(FIRST):
        block = coeff_block(msg_ref, chunk_refs[j], tails, k, rank)
        for p in range(PEERS):
            out_ref[p, j * rank : (j + 1) * rank, :] = block[p * rank : (p + 1) * rank, :]


def last_coeff_kernel(rank, msg_ref, _, *refs):
    chunk_refs, (out_ref, held_ref, sem) = refs[:-3], refs[-3:]
    tails = [msg_ref[p, NZ * rank :, :].astype(jnp.float32) for p in range(PEERS)]
    for j, k in enumerate(LAST):
        block = coeff_block(msg_ref, chunk_refs[j], tails, k, rank)
        for p in range(PEERS):
            held_ref[p, j * rank : (j + 1) * rank, :] = block[p * rank : (p + 1) * rank, :]
    start = len(FIRST) * rank
    copy = pltpu.make_async_copy(held_ref, out_ref.at[:, pl.ds(start, len(LAST) * rank), :], sem)
    copy.start()
    copy.wait()


def far_kernel(ks, z_ref, rows_ref, ranks_ref, left_ref, coeff_ref, near_ref, out_ref, spread_ref):
    z = z_ref[0]
    n_slots, rank, size = left_ref.shape
    n_rhs = coeff_ref.shape[2]
    n_clusters = near_ref.shape[0] // size
    index = lax.broadcasted_iota(jnp.int32, (rank, n_rhs), 0)
    spread_ref[...] = jnp.zeros_like(spread_ref)
    for p in range(PEERS):
        for j, k in enumerate(ks):
            slot = slot_of(z, k, p)
            block = coeff_ref[p, j * rank : (j + 1) * rank, :].astype(jnp.float32)
            block = jnp.where(index < ranks_ref[slot], block, 0.0)
            start = pl.multiple_of(slot * rank, rank)
            column = pl.multiple_of(rows_ref[slot] * n_rhs, n_rhs)
            spread_ref[pl.ds(start, rank), pl.ds(column, n_rhs)] = block.astype(jnp.bfloat16)
    far = lax.dot_general(
        left_ref[...].reshape(n_slots * rank, size),
        spread_ref[...],
        (((0,), (0,)), ((), ())),
        preferred_element_type=jnp.float32,
    )
    for c in range(n_clusters):
        rows = slice(c * size, (c + 1) * size)
        out_ref[rows, :] = near_ref[rows, :] + far[:, c * n_rhs : (c + 1) * n_rhs]


def near_kernel(y_ref, tiles_ref, *refs):
    chunk_refs, out_ref = refs[:-1], refs[-1]
    width = chunk_refs[0].shape[0]
    sign = 1 - 2 * lax.rem(y_ref[0], 2)
    total = None
    for step, chunk_ref in enumerate(chunk_refs):
        place = lax.rem(y_ref[0] + step * sign + len(chunk_refs), len(chunk_refs))
        column = pl.multiple_of(place * width, width)
        term = jnp.dot(tiles_ref[:, pl.ds(column, width)], chunk_ref[...], preferred_element_type=jnp.float32)
        total = term if total is None else total + term
    out_ref[...] = total


def swap(a, axis, size, odd):
    return lax.ppermute(a, axis, [(i, (i + (1 if i % 2 == odd else -1)) % size) for i in range(size)])


def local(n_grp, inputs, near_tiles, far_left, far_right, far_rows, far_cols, far_rank):
    n_clusters, size, width_cols = near_tiles.shape
    unknowns, n_rhs = inputs.shape
    n_slots, _, rank = far_left.shape
    z = lax.axis_index("z").astype(jnp.int32).reshape(1)

    chunks, one, two = {0: inputs}, inputs, inputs
    for step in range(1, NZ // 2 + 1):
        one = swap(one, "z", NZ, (step + 1) % 2)
        chunks[step if step % 2 else NZ - step] = one
        if step < NZ // 2:
            two = swap(two, "z", NZ, step % 2)
            chunks[NZ - step if step % 2 else step] = two
        if step == 2:
            one, two, held = lax.optimization_barrier((one, two, inputs))
            beside = [inputs, swap(held, "grp", n_grp, 0), None, swap(held, "grp", n_grp, 1)]
            beside[2] = swap(beside[3], "grp", n_grp, 0)
        elif step < NZ // 2:
            one, two = lax.optimization_barrier((one, two))

    packed = call(
        pack_kernel,
        jax.ShapeDtypeStruct((PEERS, NZ * rank + 16, size), jnp.bfloat16),
        [smem(), smem(), vmem()],
    )(z, far_cols, jnp.swapaxes(far_right, 1, 2))
    msg = lax.all_to_all(packed, PLANE, 0, 0, tiled=True)

    y = lax.axis_index("grp").astype(jnp.int32).reshape(1)
    out = jax.ShapeDtypeStruct((PEERS, NZ * rank, n_rhs), jnp.bfloat16)
    coeff = call(functools.partial(first_coeff_kernel, rank), out, [vmem()] * (1 + len(FIRST)))(
        msg, *[chunks[k] for k in FIRST]
    )
    anywhere = pl.BlockSpec(memory_space=pl.ANY)
    coeff = pl.pallas_call(
        functools.partial(last_coeff_kernel, rank),
        out_shape=out,
        in_specs=[vmem(), anywhere] + [vmem()] * len(LAST),
        out_specs=anywhere,
        scratch_shapes=[pltpu.VMEM((PEERS, len(LAST) * rank, n_rhs), jnp.bfloat16), pltpu.SemaphoreType.DMA],
        input_output_aliases={1: 0},
        compiler_params=pltpu.CompilerParams(vmem_limit_bytes=VMEM_LIMIT),
    )(msg, coeff, *[chunks[k] for k in LAST])
    back = lax.all_to_all(coeff, PLANE, 0, 0, tiled=True)

    near = call(
        near_kernel,
        jax.ShapeDtypeStruct((unknowns, n_rhs), jnp.float32),
        [smem()] + [vmem()] * (1 + n_grp),
        flops=3 * 10**10,
    )(y, near_tiles.reshape(unknowns, width_cols), *beside)
    return call(
        functools.partial(far_kernel, FIRST + LAST),
        jax.ShapeDtypeStruct((unknowns, n_rhs), jnp.float32),
        [smem(), smem(), smem(), vmem(), vmem(), vmem()],
        [pltpu.VMEM((n_slots * rank, n_clusters * n_rhs), jnp.bfloat16)],
    )(z, far_rows, far_rank, jnp.swapaxes(far_left, 1, 2), back, near)


def solution(mesh):
    n_grp = mesh.shape["grp"]
    fine = Mesh(mesh.devices.reshape(NZ, NX, NCORE, n_grp), ("z", "x", "core", "grp"))
    spec = P(("z", "x", "core", "grp"))
    return jax.shard_map(
        functools.partial(local, n_grp), mesh=fine, in_specs=(spec,) * 7, out_specs=spec, check_vma=False
    )
```

```python
import functools

import jax
import jax.numpy as jnp
from jax import lax
from jax.experimental import pallas as pl
from jax.experimental.pallas import tpu as pltpu
from jax.sharding import Mesh, PartitionSpec as P

NZ, NX, NCORE = 8, 4, 2
PEERS = NX * NCORE
PLANE = ("x", "core")
FIRST, LAST = (0, 7, 1, 6, 2, 5, 3), (4,)
VMEM_LIMIT = 16 * 1024 * 1024


def slot_of(z, k, peer):
    step = k * (1 - 2 * lax.rem(z, 2))
    return lax.rem(z + step + NZ, NZ) * PEERS + peer


def vmem():
    return pl.BlockSpec(memory_space=pltpu.VMEM)


def smem():
    return pl.BlockSpec(memory_space=pltpu.SMEM)


def call(kernel, out, in_specs, scratch=(), flops=0):
    return pl.pallas_call(
        kernel,
        out_shape=out,
        in_specs=in_specs,
        out_specs=vmem(),
        scratch_shapes=list(scratch),
        compiler_params=pltpu.CompilerParams(vmem_limit_bytes=VMEM_LIMIT),
        cost_estimate=pl.CostEstimate(flops=flops, bytes_accessed=0, transcendentals=0) if flops else None,
    )


def pack_kernel(z_ref, cols_ref, right_ref, out_ref, held_ref, sems):
    z = z_ref[0]
    _, rank, width = right_ref.shape
    copies = [pltpu.make_async_copy(cols_ref, held_ref, sems.at[NZ])]
    for k in range(NZ):
        first = pl.multiple_of(slot_of(z, k, 0), PEERS)
        copies.append(
            pltpu.make_async_copy(
                right_ref.at[pl.ds(first, PEERS)], out_ref.at[:, pl.ds(k * rank, rank), :], sems.at[k]
            )
        )
    for copy in copies:
        copy.start()
    copies[0].wait()
    row = lax.broadcasted_iota(jnp.int32, (16, width), 0)
    for p in range(PEERS):
        tail = jnp.zeros((16, width), jnp.float32)
        for k in range(NZ):
            slot = slot_of(z, k, p)
            tail = jnp.where(row == k, held_ref[slot].astype(jnp.float32), tail)
        out_ref[p, NZ * rank :, :] = tail.astype(jnp.bfloat16)
    for copy in copies[1:]:
        copy.wait()


def coeff_block(msg_ref, chunk_ref, tails, k, rank):
    size = msg_ref.shape[2]
    total = None
    for c in range(chunk_ref.shape[0] // size):
        parts = []
        for p in range(PEERS):
            pick = (tails[p][k : k + 1, :] == c).astype(jnp.bfloat16)
            parts.append(msg_ref[p, k * rank : (k + 1) * rank, :] * pick)
        term = jnp.dot(
            jnp.concatenate(parts, axis=0),
            chunk_ref[c * size : (c + 1) * size, :],
            preferred_element_type=jnp.float32,
        )
        total = term if total is None else total + term
    return total.astype(jnp.bfloat16)


def first_coeff_kernel(rank, msg_ref, *refs):
    chunk_refs, out_ref = refs[:-1], refs[-1]
    tails = [msg_ref[p, NZ * rank :, :].astype(jnp.float32) for p in range(PEERS)]
    for j, k in enumerate(FIRST):
        block = coeff_block(msg_ref, chunk_refs[j], tails, k, rank)
        for p in range(PEERS):
            out_ref[p, j * rank : (j + 1) * rank, :] = block[p * rank : (p + 1) * rank, :]


def last_coeff_kernel(rank, msg_ref, _, *refs):
    chunk_refs, (out_ref, held_ref, sem) = refs[:-3], refs[-3:]
    tails = [msg_ref[p, NZ * rank :, :].astype(jnp.float32) for p in range(PEERS)]
    for j, k in enumerate(LAST):
        block = coeff_block(msg_ref, chunk_refs[j], tails, k, rank)
        for p in range(PEERS):
            held_ref[p, j * rank : (j + 1) * rank, :] = block[p * rank : (p + 1) * rank, :]
    start = len(FIRST) * rank
    copy = pltpu.make_async_copy(held_ref, out_ref.at[:, pl.ds(start, len(LAST) * rank), :], sem)
    copy.start()
    copy.wait()


def far_kernel(ks, z_ref, rows_ref, ranks_ref, left_ref, coeff_ref, near_ref, out_ref, spread_ref):
    z = z_ref[0]
    n_slots, rank, size = left_ref.shape
    n_rhs = coeff_ref.shape[2]
    n_clusters = near_ref.shape[0] // size
    index = lax.broadcasted_iota(jnp.int32, (rank, n_rhs), 0)
    spread_ref[...] = jnp.zeros_like(spread_ref)
    for p in range(PEERS):
        for j, k in enumerate(ks):
            slot = slot_of(z, k, p)
            block = coeff_ref[p, j * rank : (j + 1) * rank, :].astype(jnp.float32)
            block = jnp.where(index < ranks_ref[slot], block, 0.0)
            start = pl.multiple_of(slot * rank, rank)
            column = pl.multiple_of(rows_ref[slot] * n_rhs, n_rhs)
            spread_ref[pl.ds(start, rank), pl.ds(column, n_rhs)] = block.astype(jnp.bfloat16)
    far = lax.dot_general(
        left_ref[...].reshape(n_slots * rank, size),
        spread_ref[...],
        (((0,), (0,)), ((), ())),
        preferred_element_type=jnp.float32,
    )
    for c in range(n_clusters):
        rows = slice(c * size, (c + 1) * size)
        out_ref[rows, :] = near_ref[rows, :] + far[:, c * n_rhs : (c + 1) * n_rhs]


def near_kernel(y_ref, tiles_ref, *refs):
    chunk_refs, out_ref = refs[:-1], refs[-1]
    width = chunk_refs[0].shape[0]
    sign = 1 - 2 * lax.rem(y_ref[0], 2)
    total = None
    for step, chunk_ref in enumerate(chunk_refs):
        place = lax.rem(y_ref[0] + step * sign + len(chunk_refs), len(chunk_refs))
        column = pl.multiple_of(place * width, width)
        term = jnp.dot(tiles_ref[:, pl.ds(column, width)], chunk_ref[...], preferred_element_type=jnp.float32)
        total = term if total is None else total + term
    out_ref[...] = total


def swap(a, axis, size, odd):
    return lax.ppermute(a, axis, [(i, (i + (1 if i % 2 == odd else -1)) % size) for i in range(size)])


def local(n_grp, inputs, near_tiles, far_left, far_right, far_rows, far_cols, far_rank):
    n_clusters, size, width_cols = near_tiles.shape
    unknowns, n_rhs = inputs.shape
    n_slots, _, rank = far_left.shape
    z = lax.axis_index("z").astype(jnp.int32).reshape(1)

    chunks, one, two = {0: inputs}, inputs, inputs
    for step in range(1, NZ // 2 + 1):
        one = swap(one, "z", NZ, (step + 1) % 2)
        chunks[step if step % 2 else NZ - step] = one
        if step < NZ // 2:
            two = swap(two, "z", NZ, step % 2)
            chunks[NZ - step if step % 2 else step] = two
        if step == 2:
            one, two, held = lax.optimization_barrier((one, two, inputs))
            beside = [inputs, swap(held, "grp", n_grp, 0), None, swap(held, "grp", n_grp, 1)]
            beside[2] = swap(beside[3], "grp", n_grp, 0)
        elif step < NZ // 2:
            one, two = lax.optimization_barrier((one, two))

    packed = call(
        pack_kernel,
        jax.ShapeDtypeStruct((PEERS, NZ * rank + 16, size), jnp.bfloat16),
        [smem()] + [pl.BlockSpec(memory_space=pl.ANY)] * 2,
        [pltpu.SMEM((n_slots,), jnp.int32), pltpu.SemaphoreType.DMA((NZ + 1,))],
    )(z, far_cols, jnp.swapaxes(far_right, 1, 2))
    msg = lax.all_to_all(packed, PLANE, 0, 0, tiled=True)

    y = lax.axis_index("grp").astype(jnp.int32).reshape(1)
    out = jax.ShapeDtypeStruct((PEERS, NZ * rank, n_rhs), jnp.bfloat16)
    coeff = call(functools.partial(first_coeff_kernel, rank), out, [vmem()] * (1 + len(FIRST)))(
        msg, *[chunks[k] for k in FIRST]
    )
    anywhere = pl.BlockSpec(memory_space=pl.ANY)
    coeff = pl.pallas_call(
        functools.partial(last_coeff_kernel, rank),
        out_shape=out,
        in_specs=[vmem(), anywhere] + [vmem()] * len(LAST),
        out_specs=anywhere,
        scratch_shapes=[pltpu.VMEM((PEERS, len(LAST) * rank, n_rhs), jnp.bfloat16), pltpu.SemaphoreType.DMA],
        input_output_aliases={1: 0},
        compiler_params=pltpu.CompilerParams(vmem_limit_bytes=VMEM_LIMIT),
    )(msg, coeff, *[chunks[k] for k in LAST])
    back = lax.all_to_all(coeff, PLANE, 0, 0, tiled=True)

    near = call(
        near_kernel,
        jax.ShapeDtypeStruct((unknowns, n_rhs), jnp.float32),
        [smem()] + [vmem()] * (1 + n_grp),
        flops=3 * 10**10,
    )(y, near_tiles.reshape(unknowns, width_cols), *beside)
    return call(
        functools.partial(far_kernel, FIRST + LAST),
        jax.ShapeDtypeStruct((unknowns, n_rhs), jnp.float32),
        [smem(), smem(), smem(), vmem(), vmem(), vmem()],
        [pltpu.VMEM((n_slots * rank, n_clusters * n_rhs), jnp.bfloat16)],
    )(z, far_rows, far_rank, jnp.swapaxes(far_left, 1, 2), back, near)


def solution(mesh):
    n_grp = mesh.shape["grp"]
    fine = Mesh(mesh.devices.reshape(NZ, NX, NCORE, n_grp), ("z", "x", "core", "grp"))
    spec = P(("z", "x", "core", "grp"))
    return jax.shard_map(
        functools.partial(local, n_grp), mesh=fine, in_specs=(spec,) * 7, out_specs=spec, check_vma=False
    )
```
